32 devices in a mesh: grp: 8 (over z, x), reg: 4 (over y, core).
Axes of the slice: x: 2, y: 2, z: 4, core: 2. Of those that a mesh axis runs over, the one named last changes fastest.
Arguments:
- orbitals: bfloat16 [4, 8, 512, 1024], P('reg', 'grp'), may hold values from -6 to 6
- occupied: bfloat16 [4, 8, 8, 512], P('reg', 'grp'), may hold values from -0.59765625 to 0.59765625
- panel_index: int32 [128], replicated, may hold values from 0 to 1023, as said below
- screening: bfloat16 [224, 512, 512], P(('grp', 'reg')), may hold values from -0.25 to 0.25
- block_region: int32 [224, 1], P(('grp', 'reg')), may hold values from 0 to 3; in each aligned block of 7 rows (0 to 6, 7 to 13, ...) at most 2 rows name the same one
- block_row: int32 [224], P(('grp', 'reg')), may hold values from 0 to 7
- block_col: int32 [224], P(('grp', 'reg')), may hold values from 0 to 7
Outputs:
- sigma: float32 [4, 128, 128], P('reg')
The draws below stay inside these ranges and needn't reach their ends.
Inputs may be any that keep to these rules, and one draw needn't show every extreme that they name: `panel_index`: the 128 indices are distinct. Among the 7 blocks of one device (aligned rows of block_region), at most 2 name the same region.
All inputs are finite; a program needn't handle non-finite values.
Results may differ from the reference program's by a relative error of at most 0.0054.
Values may be sent and summed in bfloat16 or wider, within the bound.
No kernel may reach another device: no remote copies, remote signals or barrier semaphores. Data moves between devices by JAX's collectives and lax.ppermute only.
A program may use at most 192 MiB of HBM per device.

```python
import math
import jax
import jax.numpy as jnp
import numpy as np
from jax import lax

PTS = 512
PANEL = 128
ORBS = 1024
OCC = 8
CAP = 2
NW_DEV = 7
REGIONS = 4
GRID_REG = 8
BLOCKS = 224


def draw_panel_index(key, part):
    stride = ORBS // PANEL
    offsets = jax.random.randint(key, (PANEL,), 0, stride)
    position = jnp.arange(PANEL)
    offsets = jnp.where(position == 0, 0, jnp.where(position == PANEL - 1, stride - 1, offsets))
    values = position * stride + offsets
    ranking = jax.random.permutation(jax.random.fold_in(key, 7), PANEL)
    return values[ranking].astype(jnp.int32)


def with_ends(array, rng, least, largest):
    extent = array.shape
    place = [jax.random.randint(jax.random.fold_in(rng, axis), (), 0, extent[axis]) for axis in range(len(extent))]
    array = array.at[tuple(place)].set(least)
    longest = extent.index(max(extent))
    place[longest] = (place[longest] + 1) % extent[longest]
    return array.at[tuple(place)].set(largest)


def level_of(rng, dims, split, low, top_value):
    def one(dim, shards_of):
        steps = jax.random.uniform(jax.random.fold_in(jax.random.fold_in(rng, 6), dim), (shards_of,), jnp.float32, low / len(split), top_value / len(split))
        return jnp.repeat(jnp.exp(steps), dims[dim] // shards_of).reshape((-1,) + (1,) * (len(dims) - dim - 1))

    gain = one(*split[0])
    for cut in split[1:]:
        gain = gain * one(*cut)
    return gain


def assign_block(rng, own, number, rows, number_of, top, limit, lean):
    order = jax.random.permutation(rng, number_of)
    crowded, common = portions_of(number_of, rows * top, limit, lean, True), portions_of(number_of, rows * top, limit, lean, False)
    places = jnp.arange(number_of)

    def named(tallies, offset_by):
        used = int((tallies > 0).sum())
        fixed = max(1, used // 4)
        passed = fixed + (places - fixed + offset_by * (used - fixed)) % max(1, number_of - fixed)
        return jnp.zeros((number_of,), jnp.int32).at[order[jnp.where(places < fixed, places, passed)]].set(jnp.asarray(tallies, jnp.int32))

    tallies = jnp.where(number % 4 == 0, named(crowded, number // 4), named(common, number - number // 4 - 1))
    mixed = jax.random.permutation(jax.random.fold_in(own, 3), number_of)
    giver, receiver = mixed[0:number_of // 2 * 2:2], mixed[1:number_of // 2 * 2:2]
    slack = jnp.minimum(tallies[giver] - 1, limit - tallies[receiver]) // 2
    slack = jnp.where((giver == order[0]) | (receiver == order[0]) | (tallies[receiver] == 0), 0, jnp.maximum(slack, 0))
    passed = jax.random.randint(jax.random.fold_in(own, 4), (number_of // 2,), 0, 1 << 20) % (slack + 1)
    tallies = tallies.at[giver].add(-passed).at[receiver].add(passed)
    items = jnp.searchsorted(jnp.cumsum(tallies), jnp.arange(rows * top), side="right").astype(jnp.int32)
    grid = items.reshape(top, rows).T
    grid = grid[jax.random.permutation(jax.random.fold_in(own, 1), rows)]
    offset_by = jax.random.randint(jax.random.fold_in(own, 2), (rows, 1), 0, top)
    return jnp.take_along_axis(grid, (jnp.arange(top)[None, :] + offset_by) % top, axis=1)


def portions_of(number_of, total, most, lean, full):
    loads = [(1 << 20) // math.isqrt(rank ** lean) + 1 for rank in range(1, number_of + 1)]
    largest = most if full else min(most, max(-(-total // number_of), total * loads[0] // sum(loads)))
    least = 1 if total - largest >= number_of - 1 else 0
    given, spare = [largest] + [least] * (number_of - 1), total - largest - least * (number_of - 1)
    while spare > 0:
        candidates = [i for i in range(1, number_of) if given[i] < largest] or [i for i in range(1, number_of) if given[i] < most]
        mass, left = sum([loads[i] for i in candidates]), spare
        for i in candidates:
            extra = min(most - given[i], max(1, left * loads[i] // mass), spare)
            given[i] = given[i] + extra
            spare = spare - extra
    return np.array(given)


def centred(rng, shape, spread, most, cuts=(), held_as=jnp.bfloat16):
    result = spread * jax.random.normal(rng, shape, jnp.float32)
    if cuts:
        result = result * level_of(rng, shape, cuts, -0.22, 0.18)
    return jnp.clip(result, -most, most).astype(held_as)


def setup_inputs(seed: int = 0) -> dict:
    streams_of = jax.random.split(jax.random.key(seed), 8)
    orbitals = centred(streams_of[0], (REGIONS, GRID_REG, PTS, ORBS), 1.0, 6.0, ((0, 4), (1, 8)))
    occupied = centred(streams_of[1], (REGIONS, GRID_REG, OCC, PTS), 0.1, 0.59765625, ((0, 4), (1, 8)))
    panel_index = draw_panel_index(jax.random.fold_in(streams_of[7], 71), 0)
    screening = centred(streams_of[3], (BLOCKS, PTS, PTS), PTS ** -0.5, 0.25, ((0, 32),))
    block_region_keys = jax.random.split(jax.random.fold_in(streams_of[4], 1), BLOCKS // NW_DEV)
    block_region_turns = jax.random.permutation(jax.random.fold_in(streams_of[4], 3), BLOCKS // NW_DEV)
    block_region = jax.vmap(lambda own, number: assign_block(jax.random.fold_in(streams_of[4], 2), own, number, NW_DEV, REGIONS, 1, CAP, 2))(block_region_keys, block_region_turns).reshape((BLOCKS, 1))
    block_row = with_ends(jax.random.randint(streams_of[5], (BLOCKS,), 0, GRID_REG), jax.random.fold_in(streams_of[5], 1), 0, GRID_REG - 1).astype(jnp.int32)
    block_col = with_ends(jax.random.randint(streams_of[6], (BLOCKS,), 0, GRID_REG), jax.random.fold_in(streams_of[6], 1), 0, GRID_REG - 1).astype(jnp.int32)
    return {"orbitals": orbitals, "occupied": occupied, "panel_index": panel_index, "screening": screening, "block_region": block_region, "block_row": block_row, "block_col": block_col}


def reference(orbitals, occupied, panel_index, screening, block_region, block_row, block_col):
    panel_orbs = jnp.take(orbitals, panel_index.astype(jnp.int32), axis=3)
    densities = (panel_orbs[:, :, :, None, :].astype(jnp.float32)
                 * jnp.swapaxes(occupied, 2, 3)[..., None].astype(jnp.float32)).astype(jnp.bfloat16)

    def accumulate(sigma, item):
        screen_tile, region, row_block, col_block = item
        col_pairs = densities[region, col_block].reshape(PTS, OCC * PANEL)
        screened = jnp.dot(screen_tile, col_pairs, preferred_element_type=jnp.float32).astype(jnp.bfloat16)
        row_pairs = densities[region, row_block].reshape(PTS * OCC, PANEL)
        contrib = jnp.dot(row_pairs.T, screened.reshape(PTS * OCC, PANEL), preferred_element_type=jnp.float32)
        return sigma.at[region].add(contrib), jnp.zeros((), jnp.float32)

    start_sigma = jnp.zeros((REGIONS, PANEL, PANEL), jnp.float32)
    sigma, unused = lax.scan(accumulate, start_sigma,
                             (screening, block_region[:, 0].astype(jnp.int32),
                              block_row.astype(jnp.int32), block_col.astype(jnp.int32)))
    return sigma
```

```python
import jax
import jax.numpy as jnp
from jax import lax
from jax.experimental import pallas as pl
from jax.experimental.pallas import tpu as pltpu
from jax.sharding import PartitionSpec as P

AXES = ("grp", "reg")
VMEM_LIMIT = 48 * 1024 * 1024


def pack_kernel(index_ref, orbitals_ref, occupied_ref, packed_ref):
    points, orbs = orbitals_ref.shape
    width = index_ref.shape[1]
    occ_count = occupied_ref.shape[0]
    rows = lax.broadcasted_iota(jnp.int32, (orbs, width), 0)
    chosen = jnp.where(rows == index_ref[...], 1.0, 0.0).astype(jnp.bfloat16)
    panel = jnp.dot(orbitals_ref[...], chosen, preferred_element_type=jnp.float32)
    packed_ref[:points, :] = panel.astype(jnp.bfloat16)
    occ = occupied_ref[...].astype(jnp.float32)
    slabs = [occ[:, at : at + width] for at in range(0, points, width)]
    packed_ref[points:, :] = jnp.concatenate(slabs, axis=0).astype(jnp.bfloat16)


def pack(panel_index, orbitals, occupied):
    points = orbitals.shape[0]
    width = panel_index.shape[0]
    occ_rows = occupied.shape[0] * points // width
    return pl.pallas_call(
        pack_kernel,
        out_shape=jax.ShapeDtypeStruct((points + occ_rows, width), jnp.bfloat16),
        compiler_params=pltpu.CompilerParams(vmem_limit_bytes=VMEM_LIMIT),
    )(panel_index[None, :], orbitals, occupied)


def sigma_kernel(pieces, points, occ_count, *refs):
    labels_ref, own_ref, other_ref = refs[:3]
    piece_refs = refs[3 : 3 + len(pieces)]
    out_ref, packed, blocks, piece_sems, block_sems = refs[3 + len(pieces) :]
    held = own_ref.shape[0]
    width = packed.shape[2]

    def piece_copy(n):
        slot, first, rows = pieces[n]
        return pltpu.make_async_copy(
            piece_refs[n], packed.at[slot, pl.ds(first, rows)], piece_sems.at[n]
        )

    def block_copy(source, n, at):
        return pltpu.make_async_copy(source.at[n], blocks.at[at], block_sems.at[at])

    for n in range(held):
        for source, at in ((own_ref, n), (other_ref, held + n)):

            @pl.when(labels_ref[at, 0] >= 0)
            def _():
                block_copy(source, n, at).start()

    for n in range(len(pieces)):
        piece_copy(n).start()
    out_ref[...] = jnp.zeros_like(out_ref)
    for n in range(len(pieces)):
        piece_copy(n).wait()

    def occupied_of(slot):
        rows = packed[slot, points:, :].astype(jnp.float32)
        slabs = [rows[at : at + occ_count] for at in range(0, rows.shape[0], occ_count)]
        return jnp.concatenate(slabs, axis=1).astype(jnp.bfloat16)

    for n in range(held):
        for source, at in ((own_ref, n), (other_ref, held + n)):
            place, row, col = labels_ref[at, 0], labels_ref[at, 1], labels_ref[at, 2]

            @pl.when(place >= 0)
            def _():
                block_copy(source, n, at).wait()
                overlap = lax.dot_general(
                    occupied_of(row),
                    occupied_of(col),
                    (((0,), (0,)), ((), ())),
                    preferred_element_type=jnp.float32,
                )
                dressed = (blocks[at].astype(jnp.float32) * overlap).astype(jnp.bfloat16)
                screened = jnp.dot(
                    dressed, packed[col, :points, :], preferred_element_type=jnp.float32
                ).astype(jnp.bfloat16)
                out_ref[place] += lax.dot_general(
                    packed[row, :points, :],
                    screened,
                    (((0,), (0,)), ((), ())),
                    preferred_element_type=jnp.float32,
                )


def partial_sigma(labels, own, other, pieces, arrays, slots, regions, points, occ_count):
    rows, width = arrays[0].shape
    rows = max(first + count for _, first, count in pieces)
    held = own.shape[0]
    return pl.pallas_call(
        lambda *refs: sigma_kernel(pieces, points, occ_count, *refs),
        out_shape=jax.ShapeDtypeStruct((regions, width, width), jnp.float32),
        in_specs=[pl.BlockSpec(memory_space=pltpu.SMEM)]
        + [pl.BlockSpec(memory_space=pl.ANY)] * (2 + len(arrays)),
        scratch_shapes=[
            pltpu.VMEM((slots, rows, width), jnp.bfloat16),
            pltpu.VMEM((2 * held,) + own.shape[1:], jnp.bfloat16),
            pltpu.SemaphoreType.DMA((len(arrays),)),
            pltpu.SemaphoreType.DMA((2 * held,)),
        ],
        compiler_params=pltpu.CompilerParams(vmem_limit_bytes=VMEM_LIMIT),
    )(labels, own, other, *arrays)


def swap(array, mask, count):
    return lax.ppermute(array, AXES, [(i, i ^ mask) for i in range(count)])


def gather(packed, count, first_bit):
    bits = []
    while first_bit < count:
        bits.append(first_bit)
        first_bit *= 2
    rows = packed.shape[0]
    half = rows // 32 * 16
    far = bits[2:]
    column = [(0, packed)]
    for mask in range(far[0], count, far[0]):
        column.append((mask, swap(packed, mask, count)))
    y, x = bits[0], bits[1]
    found = []
    for mask, array in column:
        over_x, over_y = swap(array, x, count), swap(array, y, count)
        found += [(mask, 0, array), (mask ^ x, 0, over_x), (mask ^ y, 0, over_y)]
        found.append((mask ^ x ^ y, 0, swap(over_x[:half], y, count)))
        found.append((mask ^ x ^ y, half, swap(over_y[half:], x, count)))
    return found


def total(values):
    while len(values) > 1:
        values = [values[n] + values[n + 1] for n in range(0, len(values), 2)]
    return values[0]


def shards(orbitals, occupied, panel_index, screening, block_region, block_row, block_col):
    groups, regions = lax.axis_size("grp"), lax.axis_size("reg")
    count = groups * regions
    me = lax.axis_index("grp") * regions + lax.axis_index("reg")
    core = lax.axis_index("reg") % 2
    points, occ_count = screening.shape[1], occupied.shape[2]

    labels = jnp.stack([block_region[:, 0], block_row, block_col], axis=1)
    both = jnp.concatenate([labels, swap(labels, 1, count)], axis=0)
    region = both[:, 0]
    place = jnp.where(region % 2 == core, (region ^ lax.axis_index("reg")) // 2, -1)
    slot = ((both[:, 1:] * regions + region[:, None]) ^ me) // 2
    labels = jnp.concatenate([place[:, None], slot], axis=1)
    other = swap(screening, 1, count)

    packed = pack(panel_index, orbitals[0, 0], occupied[0, 0])
    found = gather(packed, count, 2)
    pieces = [(mask // 2, first, array.shape[0]) for mask, first, array in found]
    sums = partial_sigma(
        labels,
        screening,
        other,
        pieces,
        [array for _, _, array in found],
        count // 2,
        regions // 2,
        points,
        occ_count,
    )
    stage = []
    for low in (0, regions):
        for mask in range(0, regions, 2):
            part = sums[mask // 2]
            stage.append(swap(part, low ^ mask, count) if low ^ mask else part)
    sigma = total(stage)
    bit = 2 * regions
    while bit < count:
        top = min(4 * bit, count)
        sigma = total([sigma] + [swap(sigma, mask, count) for mask in range(bit, top, bit)])
        bit = top
    return sigma[None]


def solution(mesh):
    in_specs = (
        P("reg", "grp", None, None),
        P("reg", "grp", None, None),
        P(),
        P(("grp", "reg"), None, None),
        P(("grp", "reg"), None),
        P(("grp", "reg")),
        P(("grp", "reg")),
    )
    out_specs = P("reg", None, None)
    return jax.shard_map(shards, mesh=mesh, in_specs=in_specs, out_specs=out_specs, check_vma=False)
```

```python
import jax
import jax.numpy as jnp
from jax import lax
from jax.experimental import pallas as pl
from jax.experimental.pallas import tpu as pltpu
from jax.sharding import PartitionSpec as P

AXES = ("grp", "reg")
CAP = 2
CHUNKS = 4
VMEM_LIMIT = 48 * 1024 * 1024


def in_hbm(array):
    return pltpu.with_memory_space_constraint(array, pltpu.HBM)


def in_vmem(array):
    return pltpu.with_memory_space_constraint(array, pltpu.VMEM)


def pack_kernel(index_hbm, orbitals_hbm, occupied_hbm, packed_ref, index, orbitals, occupied, sems):
    points, orbs = orbitals.shape
    width = index.shape[1]
    step = points // CHUNKS
    copies = [
        pltpu.make_async_copy(index_hbm, index, sems.at[CHUNKS + 1]),
        pltpu.make_async_copy(occupied_hbm, occupied, sems.at[CHUNKS]),
    ]
    for n in range(CHUNKS):
        rows = pl.ds(n * step, step)
        copies.append(pltpu.make_async_copy(orbitals_hbm.at[rows], orbitals.at[rows], sems.at[n]))
    for copy in copies:
        copy.start()
    copies[0].wait()
    numbers = lax.broadcasted_iota(jnp.int32, (orbs, width), 0)
    chosen = jnp.where(numbers == index[...], 1.0, 0.0).astype(jnp.bfloat16)
    copies[1].wait()
    occ = occupied[...].astype(jnp.float32)
    slabs = [occ[:, at : at + width] for at in range(0, points, width)]
    packed_ref[points:, :] = jnp.concatenate(slabs, axis=0).astype(jnp.bfloat16)
    for n in range(CHUNKS):
        copies[2 + n].wait()
        rows = slice(n * step, n * step + step)
        panel = jnp.dot(orbitals[rows, :], chosen, preferred_element_type=jnp.float32)
        packed_ref[rows, :] = panel.astype(jnp.bfloat16)


def pack(panel_index, orbitals, occupied):
    points = orbitals.shape[0]
    width = panel_index.shape[0]
    occ_rows = occupied.shape[0] * points // width
    return pl.pallas_call(
        pack_kernel,
        out_shape=pltpu.VMEM((points + occ_rows, width), jnp.bfloat16),
        out_specs=pl.BlockSpec(memory_space=pltpu.VMEM),
        in_specs=[pl.BlockSpec(memory_space=pltpu.HBM)] * 3,
        scratch_shapes=[
            pltpu.VMEM((1, width), jnp.int32),
            pltpu.VMEM(orbitals.shape, jnp.bfloat16),
            pltpu.VMEM(occupied.shape, jnp.bfloat16),
            pltpu.SemaphoreType.DMA((CHUNKS + 2,)),
        ],
        compiler_params=pltpu.CompilerParams(vmem_limit_bytes=VMEM_LIMIT),
    )(in_hbm(panel_index[None, :]), in_hbm(orbitals), in_hbm(occupied))


def collect_kernel(codes_ref, own_hbm, other_hbm, labels_ref, blocks_ref, sems):
    groups, regions = lax.axis_size("grp"), lax.axis_size("reg")
    reg = lax.axis_index("reg")
    me = lax.axis_index("grp") * regions + reg
    held = own_hbm.shape[0]
    slots = blocks_ref.shape[0]

    def block_copy(source, n, at):
        return pltpu.make_async_copy(source.at[n], blocks_ref.at[at], sems.at[at])

    for at in range(slots):
        labels_ref[at, 0] = -1
        labels_ref[at, 1] = 0
        labels_ref[at, 2] = 0
    used = jnp.int32(0)
    for source, first in ((own_hbm, 0), (other_hbm, held)):
        for n in range(held):
            code = codes_ref[first + n]
            region = code % regions
            row = code // regions % groups
            col = code // (regions * groups)
            wanted = (region ^ reg) % 2 == 0

            @pl.when(wanted)
            def _():
                labels_ref[used, 0] = (region ^ reg) // 2
                labels_ref[used, 1] = ((row * regions + region) ^ me) // 2
                labels_ref[used, 2] = ((col * regions + region) ^ me) // 2
                block_copy(source, n, used).start()

            used = used + wanted.astype(jnp.int32)
    for at in range(slots):

        @pl.when(at < used)
        def _():
            block_copy(own_hbm, 0, at).wait()


def collect(codes, own, other, regions):
    held = own.shape[0]
    slots = min(2 * held, 2 * CAP * regions)
    return pl.pallas_call(
        collect_kernel,
        out_shape=(
            pltpu.SMEM((slots, 3), jnp.int32),
            pltpu.VMEM((slots,) + own.shape[1:], jnp.bfloat16),
        ),
        in_specs=[pl.BlockSpec(memory_space=pltpu.SMEM)]
        + [pl.BlockSpec(memory_space=pltpu.HBM)] * 2,
        out_specs=(
            pl.BlockSpec(memory_space=pltpu.SMEM),
            pl.BlockSpec(memory_space=pltpu.VMEM),
        ),
        scratch_shapes=[pltpu.SemaphoreType.DMA((slots,))],
        compiler_params=pltpu.CompilerParams(vmem_limit_bytes=VMEM_LIMIT),
    )(codes, in_hbm(own), in_hbm(other))


def sigma_kernel(places, points, occ_count, labels_ref, blocks, *refs):
    piece_refs = refs[: len(places)]
    out_ref, packed, dressed, screened = refs[len(places) :]
    slots = blocks.shape[0]
    out_ref[...] = jnp.zeros_like(out_ref)
    for n, place in enumerate(places):
        packed[place] = piece_refs[n][...]

    def occupied_of(slot):
        rows = packed[slot, points:, :].astype(jnp.float32)
        slabs = [rows[at : at + occ_count] for at in range(0, rows.shape[0], occ_count)]
        return jnp.concatenate(slabs, axis=1).astype(jnp.bfloat16)

    transposed = (((0,), (0,)), ((), ()))
    for at in range(slots):
        row, col = labels_ref[at, 1], labels_ref[at, 2]
        overlap = lax.dot_general(
            occupied_of(row), occupied_of(col), transposed, preferred_element_type=jnp.float32
        )
        dressed[at] = (blocks[at].astype(jnp.float32) * overlap).astype(jnp.bfloat16)
    for at in range(slots):
        col = labels_ref[at, 2]
        screened[at] = jnp.dot(
            dressed[at], packed[col, :points, :], preferred_element_type=jnp.float32
        ).astype(jnp.bfloat16)
    for at in range(slots):
        place, row = labels_ref[at, 0], labels_ref[at, 1]
        product = lax.dot_general(
            packed[row, :points, :], screened[at], transposed, preferred_element_type=jnp.float32
        )
        out_ref[jnp.maximum(place, 0)] += jnp.where(place >= 0, product, 0.0)


def partial_sigma(labels, blocks, found, regions, points, occ_count):
    arrays = [array for _, array in found]
    places = [mask // 2 for mask, _ in found]
    rows, width = arrays[0].shape
    slots = blocks.shape[0]
    return pl.pallas_call(
        lambda *refs: sigma_kernel(places, points, occ_count, *refs),
        out_shape=pltpu.VMEM((regions, width, width), jnp.float32),
        in_specs=[pl.BlockSpec(memory_space=pltpu.SMEM)]
        + [pl.BlockSpec(memory_space=pltpu.VMEM)] * (1 + len(arrays)),
        out_specs=pl.BlockSpec(memory_space=pltpu.VMEM),
        scratch_shapes=[
            pltpu.VMEM((len(arrays), rows, width), jnp.bfloat16),
            pltpu.VMEM((slots, points, points), jnp.bfloat16),
            pltpu.VMEM((slots, points, width), jnp.bfloat16),
        ],
        compiler_params=pltpu.CompilerParams(vmem_limit_bytes=VMEM_LIMIT),
    )(
        pltpu.with_memory_space_constraint(labels, pltpu.SMEM),
        in_vmem(blocks),
        *[in_vmem(array) for array in arrays],
    )


def swap(array, mask, count):
    return lax.ppermute(array, AXES, [(i, i ^ mask) for i in range(count)])


def gather(packed, count, first_bit):
    bits = []
    while first_bit < count:
        bits.append(first_bit)
        first_bit *= 2
    y, x = bits[0], bits[1]
    column = [(0, packed)]
    for mask in range(bits[2], count, bits[2]):
        column.append((mask, swap(packed, mask, count)))
    found = []
    earlier = []
    for n, (mask, array) in enumerate(column):
        if n >= 2:
            array, _ = lax.optimization_barrier((array, earlier[n - 2]))
        over_x, over_y = swap(array, x, count), swap(array, y, count)
        corner = swap(over_x, y, count) if n % 2 else swap(over_y, x, count)
        earlier.append(corner)
        found += [(mask, array), (mask ^ x, over_x), (mask ^ y, over_y), (mask ^ x ^ y, corner)]
    return found


def total(values):
    while len(values) > 1:
        values = [values[n] + values[n + 1] for n in range(0, len(values), 2)]
    return values[0]


def shards(orbitals, occupied, panel_index, screening, block_region, block_row, block_col):
    groups, regions = lax.axis_size("grp"), lax.axis_size("reg")
    count = groups * regions
    points, occ_count = screening.shape[1], occupied.shape[2]

    other = swap(screening, 1, count)
    packed = pack(panel_index, orbitals[0, 0], occupied[0, 0])
    found = gather(packed, count, 2)
    codes = (block_col * groups + block_row) * regions + block_region[:, 0]
    codes = jnp.concatenate([codes, swap(codes, 1, count)])
    labels, blocks = collect(codes, screening, other, regions // 2)
    sums = partial_sigma(labels, blocks, found, regions // 2, points, occ_count)
    stage = []
    for low in (0, regions):
        for mask in range(0, regions, 2):
            part = sums[mask // 2]
            stage.append(swap(part, low ^ mask, count) if low ^ mask else part)
    sigma = total(stage)
    bit = 2 * regions
    while bit < count:
        top = min(4 * bit, count)
        sigma = total([sigma] + [swap(sigma, mask, count) for mask in range(bit, top, bit)])
        bit = top
    return sigma[None]


def solution(mesh):
    in_specs = (
        P("reg", "grp", None, None),
        P("reg", "grp", None, None),
        P(),
        P(("grp", "reg"), None, None),
        P(("grp", "reg"), None),
        P(("grp", "reg")),
        P(("grp", "reg")),
    )
    out_specs = P("reg", None, None)
    return jax.shard_map(shards, mesh=mesh, in_specs=in_specs, out_specs=out_specs, check_vma=False)
```

```python
import jax
import jax.numpy as jnp
from jax import lax
from jax.experimental import pallas as pl
from jax.experimental.pallas import tpu as pltpu
from jax.sharding import PartitionSpec as P

AXES = ("grp", "reg")
CAP = 2
CHUNKS = 4
VMEM_LIMIT = 48 * 1024 * 1024


def in_hbm(array):
    return pltpu.with_memory_space_constraint(array, pltpu.HBM)


def in_vmem(array):
    return pltpu.with_memory_space_constraint(array, pltpu.VMEM)


def pack_kernel(index_hbm, orbitals_hbm, occupied_hbm, packed_ref, index, orbitals, occupied, sems):
    points, orbs = orbitals.shape
    width = index.shape[1]
    step = points // CHUNKS
    copies = [
        pltpu.make_async_copy(index_hbm, index, sems.at[CHUNKS + 1]),
        pltpu.make_async_copy(occupied_hbm, occupied, sems.at[CHUNKS]),
    ]
    for n in range(CHUNKS):
        rows = pl.ds(n * step, step)
        copies.append(pltpu.make_async_copy(orbitals_hbm.at[rows], orbitals.at[rows], sems.at[n]))
    for copy in copies:
        copy.start()
    copies[0].wait()
    numbers = lax.broadcasted_iota(jnp.int32, (orbs, width), 0)
    chosen = jnp.where(numbers == index[...], 1.0, 0.0).astype(jnp.bfloat16)
    copies[1].wait()
    occ = occupied[...].astype(jnp.float32)
    slabs = [occ[:, at : at + width] for at in range(0, points, width)]
    packed_ref[points:, :] = jnp.concatenate(slabs, axis=0).astype(jnp.bfloat16)
    for n in range(CHUNKS):
        copies[2 + n].wait()
        rows = slice(n * step, n * step + step)
        panel = jnp.dot(orbitals[rows, :], chosen, preferred_element_type=jnp.float32)
        packed_ref[rows, :] = panel.astype(jnp.bfloat16)


def pack(panel_index, orbitals, occupied):
    points = orbitals.shape[0]
    width = panel_index.shape[0]
    occ_rows = occupied.shape[0] * points // width
    return pl.pallas_call(
        pack_kernel,
        out_shape=pltpu.VMEM((points + occ_rows, width), jnp.bfloat16),
        out_specs=pl.BlockSpec(memory_space=pltpu.VMEM),
        in_specs=[pl.BlockSpec(memory_space=pltpu.HBM)] * 3,
        scratch_shapes=[
            pltpu.VMEM((1, width), jnp.int32),
            pltpu.VMEM(orbitals.shape, jnp.bfloat16),
            pltpu.VMEM(occupied.shape, jnp.bfloat16),
            pltpu.SemaphoreType.DMA((CHUNKS + 2,)),
        ],
        cost_estimate=pl.CostEstimate(flops=4 * 10**10, bytes_accessed=0, transcendentals=0),
        compiler_params=pltpu.CompilerParams(vmem_limit_bytes=VMEM_LIMIT),
    )(in_hbm(panel_index[None, :]), in_hbm(orbitals), in_hbm(occupied))


def collect_kernel(own_codes, other_codes, own_hbm, labels_ref, blocks_ref, own, other, sems):
    groups, regions = lax.axis_size("grp"), lax.axis_size("reg")
    reg = lax.axis_index("reg")
    me = lax.axis_index("grp") * regions + reg
    held = own_hbm.shape[0]
    half = blocks_ref.shape[0]
    copies = [
        pltpu.make_async_copy(own_codes, own, sems.at[half]),
        pltpu.make_async_copy(other_codes, other, sems.at[half + 1]),
    ]

    def block_copy(n, at):
        return pltpu.make_async_copy(own_hbm.at[n], blocks_ref.at[at], sems.at[at])

    for copy in copies:
        copy.start()
    for at in range(2 * half):
        labels_ref[at, 0] = -1
        for column in range(1, 4):
            labels_ref[at, column] = 0
    for copy, codes, first in zip(copies, (own, other), (0, half)):
        copy.wait()
        used = jnp.int32(first)
        for n in range(held):
            code = codes[n]
            region = code % regions
            row = code // regions % groups
            col = code // (regions * groups)
            wanted = (region ^ reg) % 2 == 0

            @pl.when(wanted)
            def _():
                labels_ref[used, 0] = (region ^ reg) // 2
                labels_ref[used, 1] = ((row * regions + region) ^ me) // 2
                labels_ref[used, 2] = ((col * regions + region) ^ me) // 2
                labels_ref[used, 3] = n
                if first == 0:
                    block_copy(n, used).start()

            used = used + wanted.astype(jnp.int32)
        if first == 0:
            used_own = used
    for at in range(half):

        @pl.when(at < used_own)
        def _():
            block_copy(0, at).wait()


def collect(codes, own, regions):
    held = own.shape[0]
    half = min(held, CAP * regions)
    return pl.pallas_call(
        collect_kernel,
        out_shape=(
            pltpu.SMEM((2 * half, 4), jnp.int32),
            pltpu.VMEM((half,) + own.shape[1:], jnp.bfloat16),
        ),
        in_specs=[pl.BlockSpec(memory_space=pltpu.HBM)] * 3,
        out_specs=(
            pl.BlockSpec(memory_space=pltpu.SMEM),
            pl.BlockSpec(memory_space=pltpu.VMEM),
        ),
        scratch_shapes=[pltpu.SMEM((held,), jnp.int32)] * 2
        + [pltpu.SemaphoreType.DMA((half + 2,))],
        compiler_params=pltpu.CompilerParams(vmem_limit_bytes=VMEM_LIMIT),
    )(*[in_hbm(array) for array in (*codes, own)])


def sigma_kernel(places, points, occ_count, labels_ref, blocks, other, *refs):
    piece_refs = refs[: len(places)]
    out_ref, packed, dressed, screened = refs[len(places) :]
    half = blocks.shape[0]
    slots = 2 * half
    out_ref[...] = jnp.zeros_like(out_ref)
    for n, place in enumerate(places):
        packed[place] = piece_refs[n][...]

    def occupied_of(slot):
        rows = packed[slot, points:, :].astype(jnp.float32)
        slabs = [rows[at : at + occ_count] for at in range(0, rows.shape[0], occ_count)]
        return jnp.concatenate(slabs, axis=1).astype(jnp.bfloat16)

    transposed = (((0,), (0,)), ((), ()))
    for at in range(slots):
        row, col = labels_ref[at, 1], labels_ref[at, 2]
        overlap = lax.dot_general(
            occupied_of(row), occupied_of(col), transposed, preferred_element_type=jnp.float32
        )
        block = blocks[at] if at < half else other[labels_ref[at, 3]]
        dressed[at] = (block.astype(jnp.float32) * overlap).astype(jnp.bfloat16)
    for at in range(slots):
        col = labels_ref[at, 2]
        screened[at] = jnp.dot(
            dressed[at], packed[col, :points, :], preferred_element_type=jnp.float32
        ).astype(jnp.bfloat16)
    for at in range(slots):
        place, row = labels_ref[at, 0], labels_ref[at, 1]
        product = lax.dot_general(
            packed[row, :points, :], screened[at], transposed, preferred_element_type=jnp.float32
        )
        out_ref[jnp.maximum(place, 0)] += jnp.where(place >= 0, product, 0.0)


def partial_sigma(labels, blocks, other, found, regions, points, occ_count):
    arrays = [array for _, array in found]
    places = [mask // 2 for mask, _ in found]
    rows, width = arrays[0].shape
    slots = 2 * blocks.shape[0]
    return pl.pallas_call(
        lambda *refs: sigma_kernel(places, points, occ_count, *refs),
        out_shape=pltpu.VMEM((regions, width, width), jnp.float32),
        in_specs=[pl.BlockSpec(memory_space=pltpu.SMEM)]
        + [pl.BlockSpec(memory_space=pltpu.VMEM)] * (2 + len(arrays)),
        out_specs=pl.BlockSpec(memory_space=pltpu.VMEM),
        scratch_shapes=[
            pltpu.VMEM((len(arrays), rows, width), jnp.bfloat16),
            pltpu.VMEM((slots, points, points), jnp.bfloat16),
            pltpu.VMEM((slots, points, width), jnp.bfloat16),
        ],
        compiler_params=pltpu.CompilerParams(vmem_limit_bytes=VMEM_LIMIT),
    )(
        pltpu.with_memory_space_constraint(labels, pltpu.SMEM),
        in_vmem(blocks),
        in_vmem(other),
        *[in_vmem(array) for array in arrays],
    )


def swap(array, mask, count):
    return lax.ppermute(array, AXES, [(i, i ^ mask) for i in range(count)])


def gather(packed, count, tied):
    y, x, near = 2, 4, 8
    far = [1 << n for n in range(3, count.bit_length() - 1)]
    column = {0: packed, far[-1]: swap(packed, far[-1], count)}
    column[far[-1]], tied = lax.optimization_barrier((column[far[-1]], tied))
    for bit in reversed(far[:-1]):
        for mask in list(column):
            column[mask ^ bit] = swap(column[mask], bit, count)
    found = dict(column)
    for mask in sorted(column):
        if mask & near and mask != near:
            over_x, over_y = (swap(found[mask ^ near ^ bit], near, count) for bit in (x, y))
        else:
            over_x, over_y = (swap(column[mask], bit, count) for bit in (x, y))
        corner = swap(over_x, y, count) if mask & near else swap(over_y, x, count)
        found.update({mask ^ x: over_x, mask ^ y: over_y, mask ^ x ^ y: corner})
    return sorted(found.items()), tied


def total(values):
    while len(values) > 1:
        values = [values[n] + values[n + 1] for n in range(0, len(values), 2)]
    return values[0]


def shards(orbitals, occupied, panel_index, screening, block_region, block_row, block_col):
    groups, regions = lax.axis_size("grp"), lax.axis_size("reg")
    count = groups * regions
    points, occ_count = screening.shape[1], occupied.shape[2]

    other = swap(screening, 1, count)
    codes = (block_col * groups + block_row) * regions + block_region[:, 0]
    codes = (codes, swap(codes, 1, count))
    packed = pack(panel_index, orbitals[0, 0], occupied[0, 0])
    packed, codes = lax.optimization_barrier((packed, codes))
    found, (codes, other) = gather(packed, count, (codes, other))
    labels, blocks = collect(codes, screening, regions // 2)
    sums = partial_sigma(labels, blocks, other, found, regions // 2, points, occ_count)
    stage = []
    for low in (0, regions):
        for mask in range(0, regions, 2):
            part = sums[mask // 2]
            stage.append(swap(part, low ^ mask, count) if low ^ mask else part)
    sigma = total(stage)
    bit = 2 * regions
    while bit < count:
        top = min(4 * bit, count)
        sigma = total([sigma] + [swap(sigma, mask, count) for mask in range(bit, top, bit)])
        bit = top
    return sigma[None]


def solution(mesh):
    in_specs = (
        P("reg", "grp", None, None),
        P("reg", "grp", None, None),
        P(),
        P(("grp", "reg"), None, None),
        P(("grp", "reg"), None),
        P(("grp", "reg")),
        P(("grp", "reg")),
    )
    out_specs = P("reg", None, None)
    return jax.shard_map(shards, mesh=mesh, in_specs=in_specs, out_specs=out_specs, check_vma=False)
```

```python
import jax
import jax.numpy as jnp
from jax import lax
from jax.experimental import pallas as pl
from jax.experimental.pallas import tpu as pltpu
from jax.sharding import PartitionSpec as P

AXES = ("grp", "reg")
CAP = 2
CHUNKS = 2
VMEM_LIMIT = 48 * 1024 * 1024


def in_hbm(array):
    return pltpu.with_memory_space_constraint(array, pltpu.HBM)


def in_vmem(array):
    return pltpu.with_memory_space_constraint(array, pltpu.VMEM)


def pack_kernel(index_hbm, orbitals_hbm, occupied_hbm, packed_ref, index, orbitals, occupied, sems):
    points, orbs = orbitals.shape
    width = index.shape[1]
    step = points // CHUNKS
    copies = [
        pltpu.make_async_copy(index_hbm, index, sems.at[CHUNKS + 1]),
        pltpu.make_async_copy(occupied_hbm, occupied, sems.at[CHUNKS]),
    ]
    for n in range(CHUNKS):
        rows = pl.ds(n * step, step)
        copies.append(pltpu.make_async_copy(orbitals_hbm.at[rows], orbitals.at[rows], sems.at[n]))
    for copy in copies:
        copy.start()
    copies[0].wait()
    numbers = lax.broadcasted_iota(jnp.int32, (orbs, width), 0)
    chosen = jnp.where(numbers == index[...], 1.0, 0.0).astype(jnp.bfloat16)
    copies[1].wait()
    occ = occupied[...].astype(jnp.float32)
    slabs = [occ[:, at : at + width] for at in range(0, points, width)]
    packed_ref[points:, :] = jnp.concatenate(slabs, axis=0).astype(jnp.bfloat16)
    for n in range(CHUNKS):
        copies[2 + n].wait()
        rows = slice(n * step, n * step + step)
        panel = jnp.dot(orbitals[rows, :], chosen, preferred_element_type=jnp.float32)
        packed_ref[rows, :] = panel.astype(jnp.bfloat16)


def pack(panel_index, orbitals, occupied):
    points = orbitals.shape[0]
    width = panel_index.shape[0]
    occ_rows = occupied.shape[0] * points // width
    return pl.pallas_call(
        pack_kernel,
        out_shape=pltpu.VMEM((points + occ_rows, width), jnp.bfloat16),
        out_specs=pl.BlockSpec(memory_space=pltpu.VMEM),
        in_specs=[pl.BlockSpec(memory_space=pltpu.HBM)] * 3,
        scratch_shapes=[
            pltpu.VMEM((1, width), jnp.int32),
            pltpu.VMEM(orbitals.shape, jnp.bfloat16),
            pltpu.VMEM(occupied.shape, jnp.bfloat16),
            pltpu.SemaphoreType.DMA((CHUNKS + 2,)),
        ],
        cost_estimate=pl.CostEstimate(flops=4 * 10**10, bytes_accessed=0, transcendentals=0),
        compiler_params=pltpu.CompilerParams(vmem_limit_bytes=VMEM_LIMIT),
    )(in_hbm(panel_index[None, :]), in_hbm(orbitals), in_hbm(occupied))


def collect_kernel(own_codes, other_codes, own_hbm, labels_ref, blocks_ref, own, other, sems):
    groups, regions = lax.axis_size("grp"), lax.axis_size("reg")
    reg = lax.axis_index("reg")
    me = lax.axis_index("grp") * regions + reg
    held = own_hbm.shape[0]
    half = blocks_ref.shape[0]
    copies = [
        pltpu.make_async_copy(own_codes, own, sems.at[half]),
        pltpu.make_async_copy(other_codes, other, sems.at[half + 1]),
    ]

    def block_copy(n, at):
        return pltpu.make_async_copy(own_hbm.at[n], blocks_ref.at[at], sems.at[at])

    for copy in copies:
        copy.start()
    for at in range(2 * half):
        labels_ref[at, 0] = -1
        for column in range(1, 4):
            labels_ref[at, column] = 0
    for copy, codes, first in zip(copies, (own, other), (0, half)):
        copy.wait()
        used = jnp.int32(first)
        for n in range(held):
            code = codes[n]
            region = code % regions
            row = code // regions % groups
            col = code // (regions * groups)
            wanted = (region ^ reg) % 2 == 0

            @pl.when(wanted)
            def _():
                labels_ref[used, 0] = (region ^ reg) // 2
                labels_ref[used, 1] = ((row * regions + region) ^ me) // 2
                labels_ref[used, 2] = ((col * regions + region) ^ me) // 2
                labels_ref[used, 3] = n
                if first == 0:
                    block_copy(n, used).start()

            used = used + wanted.astype(jnp.int32)
        if first == 0:
            used_own = used
    for at in range(half):

        @pl.when(at < used_own)
        def _():
            block_copy(0, at).wait()


def collect(codes, own, regions):
    held = own.shape[0]
    half = min(held, CAP * regions)
    return pl.pallas_call(
        collect_kernel,
        out_shape=(
            pltpu.SMEM((2 * half, 4), jnp.int32),
            pltpu.VMEM((half,) + own.shape[1:], jnp.bfloat16),
        ),
        in_specs=[pl.BlockSpec(memory_space=pltpu.HBM)] * 3,
        out_specs=(
            pl.BlockSpec(memory_space=pltpu.SMEM),
            pl.BlockSpec(memory_space=pltpu.VMEM),
        ),
        scratch_shapes=[pltpu.SMEM((held,), jnp.int32)] * 2
        + [pltpu.SemaphoreType.DMA((half + 2,))],
        compiler_params=pltpu.CompilerParams(vmem_limit_bytes=VMEM_LIMIT),
    )(*[in_hbm(array) for array in (*codes, own)])


def sigma_kernel(places, points, occ_count, labels_ref, blocks, other, *refs):
    piece_refs = refs[: len(places)]
    out_ref, packed, dressed, screened = refs[len(places) :]
    half = blocks.shape[0]
    slots = 2 * half
    out_ref[...] = jnp.zeros_like(out_ref)
    for n, place in enumerate(places):
        packed[place] = piece_refs[n][...]

    def occupied_of(slot):
        rows = packed[slot, points:, :].astype(jnp.float32)
        slabs = [rows[at : at + occ_count] for at in range(0, rows.shape[0], occ_count)]
        return jnp.concatenate(slabs, axis=1).astype(jnp.bfloat16)

    transposed = (((0,), (0,)), ((), ()))
    for at in range(slots):
        row, col = labels_ref[at, 1], labels_ref[at, 2]
        overlap = lax.dot_general(
            occupied_of(row), occupied_of(col), transposed, preferred_element_type=jnp.float32
        )
        block = blocks[at] if at < half else other[labels_ref[at, 3]]
        dressed[at] = (block.astype(jnp.float32) * overlap).astype(jnp.bfloat16)
    for at in range(slots):
        col = labels_ref[at, 2]
        screened[at] = jnp.dot(
            dressed[at], packed[col, :points, :], preferred_element_type=jnp.float32
        ).astype(jnp.bfloat16)
    for at in range(slots):
        place, row = labels_ref[at, 0], labels_ref[at, 1]
        product = lax.dot_general(
            packed[row, :points, :], screened[at], transposed, preferred_element_type=jnp.float32
        )
        out_ref[jnp.maximum(place, 0)] += jnp.where(place >= 0, product, 0.0)


def partial_sigma(labels, blocks, other, found, regions, points, occ_count):
    arrays = [array for _, array in found]
    places = [mask // 2 for mask, _ in found]
    rows, width = arrays[0].shape
    slots = 2 * blocks.shape[0]
    return pl.pallas_call(
        lambda *refs: sigma_kernel(places, points, occ_count, *refs),
        out_shape=pltpu.VMEM((regions, width, width), jnp.float32),
        in_specs=[pl.BlockSpec(memory_space=pltpu.SMEM)]
        + [pl.BlockSpec(memory_space=pltpu.VMEM)] * (2 + len(arrays)),
        out_specs=pl.BlockSpec(memory_space=pltpu.VMEM),
        scratch_shapes=[
            pltpu.VMEM((len(arrays), rows, width), jnp.bfloat16),
            pltpu.VMEM((slots, points, points), jnp.bfloat16),
            pltpu.VMEM((slots, points, width), jnp.bfloat16),
        ],
        compiler_params=pltpu.CompilerParams(vmem_limit_bytes=VMEM_LIMIT),
    )(
        pltpu.with_memory_space_constraint(labels, pltpu.SMEM),
        in_vmem(blocks),
        in_vmem(other),
        *[in_vmem(array) for array in arrays],
    )


def swap(array, mask, count):
    return lax.ppermute(array, AXES, [(i, i ^ mask) for i in range(count)])


def gather(packed, count, blocks, codes):
    y, x, near = 2, 4, 8
    far = [1 << n for n in range(3, count.bit_length() - 1)]
    column = {0: packed}
    for bit in reversed(far):
        for mask, array in list(column.items()):
            if bit == near and mask == far[-1]:
                array, blocks = lax.optimization_barrier((array, blocks))
            column[mask ^ bit] = swap(array, bit, count)
    found = dict(column)
    for mask in sorted(column):
        if mask & near and mask != near:
            over_x, over_y = (swap(found[mask ^ near ^ bit], near, count) for bit in (x, y))
        else:
            over_x, over_y = (swap(column[mask], bit, count) for bit in (x, y))
        sent = over_x if mask & near else over_y
        if mask == 0:
            sent, codes = lax.optimization_barrier((sent, codes))
        corner = swap(sent, y if mask & near else x, count)
        found.update({mask ^ x: over_x, mask ^ y: over_y, mask ^ x ^ y: corner})
    return sorted(found.items()), blocks, codes


def total(values):
    while len(values) > 1:
        values = [values[n] + values[n + 1] for n in range(0, len(values), 2)]
    return values[0]


def shards(orbitals, occupied, panel_index, screening, block_region, block_row, block_col):
    groups, regions = lax.axis_size("grp"), lax.axis_size("reg")
    count = groups * regions
    points, occ_count = screening.shape[1], occupied.shape[2]

    other = swap(screening, 1, count)
    codes = (block_col * groups + block_row) * regions + block_region[:, 0]
    codes = (codes, swap(codes, 1, count))
    packed = pack(panel_index, orbitals[0, 0], occupied[0, 0])
    found, other, codes = gather(packed, count, other, codes)
    labels, blocks = collect(codes, screening, regions // 2)
    sums = partial_sigma(labels, blocks, other, found, regions // 2, points, occ_count)
    stage = []
    for low in (0, regions):
        for mask in range(0, regions, 2):
            part = sums[mask // 2]
            stage.append(swap(part, low ^ mask, count) if low ^ mask else part)
    sigma = total(stage)
    bit = 2 * regions
    while bit < count:
        top = min(4 * bit, count)
        sigma = total([sigma] + [swap(sigma, mask, count) for mask in range(bit, top, bit)])
        bit = top
    return sigma[None]


def solution(mesh):
    in_specs = (
        P("reg", "grp", None, None),
        P("reg", "grp", None, None),
        P(),
        P(("grp", "reg"), None, None),
        P(("grp", "reg"), None),
        P(("grp", "reg")),
        P(("grp", "reg")),
    )
    out_specs = P("reg", None, None)
    return jax.shard_map(shards, mesh=mesh, in_specs=in_specs, out_specs=out_specs, check_vma=False)
```

```python
import jax
import jax.numpy as jnp
from jax import lax
from jax.experimental import pallas as pl
from jax.experimental.pallas import tpu as pltpu
from jax.sharding import PartitionSpec as P

AXES = ("grp", "reg")
CAP = 2
CHUNKS = 2
VMEM_LIMIT = 48 * 1024 * 1024


def in_hbm(array):
    return pltpu.with_memory_space_constraint(array, pltpu.HBM)


def in_vmem(array):
    return pltpu.with_memory_space_constraint(array, pltpu.VMEM)


def pack_kernel(index_hbm, orbitals_hbm, occupied_hbm, packed_ref, index, orbitals, occupied, sems):
    points, orbs = orbitals.shape
    width = index.shape[1]
    step = points // CHUNKS
    copies = [
        pltpu.make_async_copy(index_hbm, index, sems.at[CHUNKS + 1]),
        pltpu.make_async_copy(occupied_hbm, occupied, sems.at[CHUNKS]),
    ]
    for n in range(CHUNKS):
        rows = pl.ds(n * step, step)
        copies.append(pltpu.make_async_copy(orbitals_hbm.at[rows], orbitals.at[rows], sems.at[n]))
    for copy in copies:
        copy.start()
    copies[0].wait()
    numbers = lax.broadcasted_iota(jnp.int32, (orbs, width), 0)
    chosen = jnp.where(numbers == index[...], 1.0, 0.0).astype(jnp.bfloat16)
    copies[1].wait()
    occ = occupied[...].astype(jnp.float32)
    slabs = [occ[:, at : at + width] for at in range(0, points, width)]
    packed_ref[points:, :] = jnp.concatenate(slabs, axis=0).astype(jnp.bfloat16)
    for n in range(CHUNKS):
        copies[2 + n].wait()
        rows = slice(n * step, n * step + step)
        panel = jnp.dot(orbitals[rows, :], chosen, preferred_element_type=jnp.float32)
        packed_ref[rows, :] = panel.astype(jnp.bfloat16)


def pack(panel_index, orbitals, occupied):
    points = orbitals.shape[0]
    width = panel_index.shape[0]
    occ_rows = occupied.shape[0] * points // width
    return pl.pallas_call(
        pack_kernel,
        out_shape=pltpu.VMEM((points + occ_rows, width), jnp.bfloat16),
        out_specs=pl.BlockSpec(memory_space=pltpu.VMEM),
        in_specs=[pl.BlockSpec(memory_space=pltpu.HBM)] * 3,
        scratch_shapes=[
            pltpu.VMEM((1, width), jnp.int32),
            pltpu.VMEM(orbitals.shape, jnp.bfloat16),
            pltpu.VMEM(occupied.shape, jnp.bfloat16),
            pltpu.SemaphoreType.DMA((CHUNKS + 2,)),
        ],
        compiler_params=pltpu.CompilerParams(vmem_limit_bytes=VMEM_LIMIT),
    )(in_hbm(panel_index[None, :]), in_hbm(orbitals), in_hbm(occupied))


def collect_kernel(own_codes, other_codes, own_hbm, labels_ref, blocks_ref, own, other, sems):
    groups, regions = lax.axis_size("grp"), lax.axis_size("reg")
    reg = lax.axis_index("reg")
    me = lax.axis_index("grp") * regions + reg
    held = own_hbm.shape[0]
    half = blocks_ref.shape[0]
    copies = [
        pltpu.make_async_copy(own_codes, own, sems.at[half]),
        pltpu.make_async_copy(other_codes, other, sems.at[half + 1]),
    ]

    def block_copy(n, at):
        return pltpu.make_async_copy(own_hbm.at[n], blocks_ref.at[at], sems.at[at])

    for copy in copies:
        copy.start()
    for at in range(2 * half):
        labels_ref[at, 0] = -1
        for column in range(1, 4):
            labels_ref[at, column] = 0
    for copy, codes, first in zip(copies, (own, other), (0, half)):
        copy.wait()
        used = jnp.int32(first)
        for n in range(held):
            code = codes[n]
            region = code % regions
            row = code // regions % groups
            col = code // (regions * groups)
            wanted = (region ^ reg) % 2 == 0

            @pl.when(wanted)
            def _():
                labels_ref[used, 0] = (region ^ reg) // 2
                labels_ref[used, 1] = ((row * regions + region) ^ me) // 2
                labels_ref[used, 2] = ((col * regions + region) ^ me) // 2
                labels_ref[used, 3] = n
                if first == 0:
                    block_copy(n, used).start()

            used = used + wanted.astype(jnp.int32)
        if first == 0:
            used_own = used
    for at in range(half):

        @pl.when(at < used_own)
        def _():
            block_copy(0, at).wait()


def collect(codes, own, regions):
    held = own.shape[0]
    half = min(held, CAP * regions)
    return pl.pallas_call(
        collect_kernel,
        out_shape=(
            pltpu.SMEM((2 * half, 4), jnp.int32),
            pltpu.VMEM((half,) + own.shape[1:], jnp.bfloat16),
        ),
        in_specs=[pl.BlockSpec(memory_space=pltpu.HBM)] * 3,
        out_specs=(
            pl.BlockSpec(memory_space=pltpu.SMEM),
            pl.BlockSpec(memory_space=pltpu.VMEM),
        ),
        scratch_shapes=[pltpu.SMEM((held,), jnp.int32)] * 2
        + [pltpu.SemaphoreType.DMA((half + 2,))],
        compiler_params=pltpu.CompilerParams(vmem_limit_bytes=VMEM_LIMIT),
    )(*[in_hbm(array) for array in (*codes, own)])


def sigma_kernel(places, points, occ_count, labels_ref, blocks, other, *refs):
    piece_refs = refs[: len(places)]
    out_ref, packed, dressed, screened = refs[len(places) :]
    half = blocks.shape[0]
    slots = 2 * half
    out_ref[...] = jnp.zeros_like(out_ref)
    for n, place in enumerate(places):
        packed[place] = piece_refs[n][...]

    def occupied_of(slot):
        rows = packed[slot, points:, :].astype(jnp.float32)
        slabs = [rows[at : at + occ_count] for at in range(0, rows.shape[0], occ_count)]
        return jnp.concatenate(slabs, axis=1).astype(jnp.bfloat16)

    transposed = (((0,), (0,)), ((), ()))
    for at in range(slots):
        row, col = labels_ref[at, 1], labels_ref[at, 2]
        overlap = lax.dot_general(
            occupied_of(row), occupied_of(col), transposed, preferred_element_type=jnp.float32
        )
        block = blocks[at] if at < half else other[labels_ref[at, 3]]
        dressed[at] = (block.astype(jnp.float32) * overlap).astype(jnp.bfloat16)
    for at in range(slots):
        col = labels_ref[at, 2]
        screened[at] = jnp.dot(
            dressed[at], packed[col, :points, :], preferred_element_type=jnp.float32
        ).astype(jnp.bfloat16)
    for at in range(slots):
        place, row = labels_ref[at, 0], labels_ref[at, 1]
        product = lax.dot_general(
            packed[row, :points, :], screened[at], transposed, preferred_element_type=jnp.float32
        )
        out_ref[jnp.maximum(place, 0)] += jnp.where(place >= 0, product, 0.0)


def partial_sigma(labels, blocks, other, found, regions, points, occ_count):
    arrays = [array for _, array in found]
    places = [mask // 2 for mask, _ in found]
    rows, width = arrays[0].shape
    slots = 2 * blocks.shape[0]
    return pl.pallas_call(
        lambda *refs: sigma_kernel(places, points, occ_count, *refs),
        out_shape=pltpu.VMEM((regions, width, width), jnp.float32),
        in_specs=[pl.BlockSpec(memory_space=pltpu.SMEM)]
        + [pl.BlockSpec(memory_space=pltpu.VMEM)] * (2 + len(arrays)),
        out_specs=pl.BlockSpec(memory_space=pltpu.VMEM),
        scratch_shapes=[
            pltpu.VMEM((len(arrays), rows, width), jnp.bfloat16),
            pltpu.VMEM((slots, points, points), jnp.bfloat16),
            pltpu.VMEM((slots, points, width), jnp.bfloat16),
        ],
        compiler_params=pltpu.CompilerParams(vmem_limit_bytes=VMEM_LIMIT),
    )(
        pltpu.with_memory_space_constraint(labels, pltpu.SMEM),
        in_vmem(blocks),
        in_vmem(other),
        *[in_vmem(array) for array in arrays],
    )


def swap(array, mask, count):
    return lax.ppermute(array, AXES, [(i, i ^ mask) for i in range(count)])


def gather(packed, count, blocks, codes):
    y, x, near = 2, 4, 8
    far = [1 << n for n in range(3, count.bit_length() - 1)]
    column = {0: packed}
    for bit in reversed(far):
        for mask, array in list(column.items()):
            if bit == near and mask == far[-1]:
                array, blocks = lax.optimization_barrier((array, blocks))
            column[mask ^ bit] = swap(array, bit, count)
    found = dict(column)
    for mask in sorted(column):
        if mask & near and mask != near:
            over_x, over_y = (swap(found[mask ^ near ^ bit], near, count) for bit in (x, y))
        else:
            over_x, over_y = (swap(column[mask], bit, count) for bit in (x, y))
        sent = over_x if mask & near else over_y
        if mask == 0:
            sent, codes = lax.optimization_barrier((sent, codes))
        corner = swap(sent, y if mask & near else x, count)
        found.update({mask ^ x: over_x, mask ^ y: over_y, mask ^ x ^ y: corner})
    return sorted(found.items()), blocks, codes


def total(values):
    while len(values) > 1:
        values = [values[n] + values[n + 1] for n in range(0, len(values), 2)]
    return values[0]


def shards(orbitals, occupied, panel_index, screening, block_region, block_row, block_col):
    groups, regions = lax.axis_size("grp"), lax.axis_size("reg")
    count = groups * regions
    points, occ_count = screening.shape[1], occupied.shape[2]

    other = swap(screening, 1, count)
    codes = (block_col * groups + block_row) * regions + block_region[:, 0]
    codes = (codes, swap(codes, 1, count))
    packed = pack(panel_index, orbitals[0, 0], occupied[0, 0])
    found, other, codes = gather(packed, count, other, codes)
    labels, blocks = collect(codes, screening, regions // 2)
    sums = partial_sigma(labels, blocks, other, found, regions // 2, points, occ_count)
    top = count // 2
    stage = []
    for far in (0, top):
        for mask in range(0, regions, 2):
            part = sums[mask // 2]
            stage.append(swap(part, far ^ mask, count) if far ^ mask else part)
    sigma = total(stage)
    bit = regions
    while bit < top:
        end = min(4 * bit, top)
        sigma = total([sigma] + [swap(sigma, mask, count) for mask in range(bit, end, bit)])
        bit = end
    return sigma[None]


def solution(mesh):
    in_specs = (
        P("reg", "grp", None, None),
        P("reg", "grp", None, None),
        P(),
        P(("grp", "reg"), None, None),
        P(("grp", "reg"), None),
        P(("grp", "reg")),
        P(("grp", "reg")),
    )
    out_specs = P("reg", None, None)
    return jax.shard_map(shards, mesh=mesh, in_specs=in_specs, out_specs=out_specs, check_vma=False)
```

```python
import jax
import jax.numpy as jnp
from jax import lax
from jax.experimental import pallas as pl
from jax.experimental.pallas import tpu as pltpu
from jax.sharding import PartitionSpec as P

AXES = ("grp", "reg")
CAP = 2
CHUNKS = 2
VMEM_LIMIT = 48 * 1024 * 1024


def in_hbm(array):
    return pltpu.with_memory_space_constraint(array, pltpu.HBM)


def in_vmem(array):
    return pltpu.with_memory_space_constraint(array, pltpu.VMEM)


def pack_kernel(index_hbm, orbitals_hbm, occupied, packed_ref, index, orbitals, sems):
    points, orbs = orbitals.shape
    width = index.shape[1]
    step = points // CHUNKS
    copies = [pltpu.make_async_copy(index_hbm, index, sems.at[CHUNKS])]
    for n in range(CHUNKS):
        rows = pl.ds(n * step, step)
        copies.append(pltpu.make_async_copy(orbitals_hbm.at[rows], orbitals.at[rows], sems.at[n]))
    for copy in copies:
        copy.start()
    copies[0].wait()
    numbers = lax.broadcasted_iota(jnp.int32, (orbs, width), 0)
    chosen = jnp.where(numbers == index[...], 1.0, 0.0).astype(jnp.bfloat16)
    occ = occupied[...].astype(jnp.float32)
    slabs = [occ[:, at : at + width] for at in range(0, points, width)]
    packed_ref[points:, :] = jnp.concatenate(slabs, axis=0).astype(jnp.bfloat16)
    for n in range(CHUNKS):
        copies[1 + n].wait()
        rows = slice(n * step, n * step + step)
        panel = jnp.dot(orbitals[rows, :], chosen, preferred_element_type=jnp.float32)
        packed_ref[rows, :] = panel.astype(jnp.bfloat16)


def pack(panel_index, orbitals, occupied):
    points = orbitals.shape[0]
    width = panel_index.shape[0]
    occ_rows = occupied.shape[0] * points // width
    return pl.pallas_call(
        pack_kernel,
        out_shape=pltpu.VMEM((points + occ_rows, width), jnp.bfloat16),
        in_specs=[pl.BlockSpec(memory_space=pltpu.HBM)] * 2
        + [pl.BlockSpec(memory_space=pltpu.VMEM)],
        out_specs=pl.BlockSpec(memory_space=pltpu.VMEM),
        scratch_shapes=[
            pltpu.VMEM((1, width), jnp.int32),
            pltpu.VMEM(orbitals.shape, jnp.bfloat16),
            pltpu.SemaphoreType.DMA((CHUNKS + 1,)),
        ],
        compiler_params=pltpu.CompilerParams(vmem_limit_bytes=VMEM_LIMIT),
    )(in_hbm(panel_index[None, :]), in_hbm(orbitals), occupied)


def collect_kernel(own_codes, other_codes, own_hbm, labels_ref, blocks_ref, own, other, sems):
    groups, regions = lax.axis_size("grp"), lax.axis_size("reg")
    reg = lax.axis_index("reg")
    me = lax.axis_index("grp") * regions + reg
    held = own_hbm.shape[0]
    half = blocks_ref.shape[0]
    copies = [
        pltpu.make_async_copy(own_codes, own, sems.at[half]),
        pltpu.make_async_copy(other_codes, other, sems.at[half + 1]),
    ]

    def block_copy(n, at):
        return pltpu.make_async_copy(own_hbm.at[n], blocks_ref.at[at], sems.at[at])

    for copy in copies:
        copy.start()
    for at in range(2 * half):
        labels_ref[at, 0] = -1
        for column in range(1, 4):
            labels_ref[at, column] = 0
    for copy, codes, first in zip(copies, (own, other), (0, half)):
        copy.wait()
        used = jnp.int32(first)
        for n in range(held):
            code = codes[n]
            region = code % regions
            row = code // regions % groups
            col = code // (regions * groups)
            wanted = (region ^ reg) % 2 == 0

            @pl.when(wanted)
            def _():
                labels_ref[used, 0] = (region ^ reg) // 2
                labels_ref[used, 1] = ((row * regions + region) ^ me) // 2
                labels_ref[used, 2] = ((col * regions + region) ^ me) // 2
                labels_ref[used, 3] = n
                if first == 0:
                    block_copy(n, used).start()

            used = used + wanted.astype(jnp.int32)
        if first == 0:
            used_own = used
    for at in range(half):

        @pl.when(at < used_own)
        def _():
            block_copy(0, at).wait()


def collect(codes, own, regions):
    held = own.shape[0]
    half = min(held, CAP * regions)
    return pl.pallas_call(
        collect_kernel,
        out_shape=(
            pltpu.SMEM((2 * half, 4), jnp.int32),
            pltpu.VMEM((half,) + own.shape[1:], jnp.bfloat16),
        ),
        in_specs=[pl.BlockSpec(memory_space=pltpu.HBM)] * 3,
        out_specs=(
            pl.BlockSpec(memory_space=pltpu.SMEM),
            pl.BlockSpec(memory_space=pltpu.VMEM),
        ),
        scratch_shapes=[pltpu.SMEM((held,), jnp.int32)] * 2
        + [pltpu.SemaphoreType.DMA((half + 2,))],
        compiler_params=pltpu.CompilerParams(vmem_limit_bytes=VMEM_LIMIT),
    )(*[in_hbm(array) for array in (*codes, own)])


def sigma_kernel(places, points, occ_count, labels_ref, blocks, other, *refs):
    piece_refs = refs[: len(places)]
    out_ref, packed, dressed, screened = refs[len(places) :]
    half = blocks.shape[0]
    slots = 2 * half
    out_ref[...] = jnp.zeros_like(out_ref)
    for n, place in enumerate(places):
        packed[place] = piece_refs[n][...]

    def occupied_of(slot):
        rows = packed[slot, points:, :].astype(jnp.float32)
        slabs = [rows[at : at + occ_count] for at in range(0, rows.shape[0], occ_count)]
        return jnp.concatenate(slabs, axis=1).astype(jnp.bfloat16)

    transposed = (((0,), (0,)), ((), ()))
    for at in range(slots):
        row, col = labels_ref[at, 1], labels_ref[at, 2]
        overlap = lax.dot_general(
            occupied_of(row), occupied_of(col), transposed, preferred_element_type=jnp.float32
        )
        block = blocks[at] if at < half else other[labels_ref[at, 3]]
        dressed[at] = (block.astype(jnp.float32) * overlap).astype(jnp.bfloat16)
    for at in range(slots):
        col = labels_ref[at, 2]
        screened[at] = jnp.dot(
            dressed[at], packed[col, :points, :], preferred_element_type=jnp.float32
        ).astype(jnp.bfloat16)
    for at in range(slots):
        place, row = labels_ref[at, 0], labels_ref[at, 1]
        product = lax.dot_general(
            packed[row, :points, :], screened[at], transposed, preferred_element_type=jnp.float32
        )
        out_ref[jnp.maximum(place, 0)] += jnp.where(place >= 0, product, 0.0)


def partial_sigma(labels, blocks, other, found, regions, points, occ_count):
    arrays = [array for _, array in found]
    places = [mask // 2 for mask, _ in found]
    rows, width = arrays[0].shape
    slots = 2 * blocks.shape[0]
    return pl.pallas_call(
        lambda *refs: sigma_kernel(places, points, occ_count, *refs),
        out_shape=pltpu.VMEM((regions, width, width), jnp.float32),
        in_specs=[pl.BlockSpec(memory_space=pltpu.SMEM)]
        + [pl.BlockSpec(memory_space=pltpu.VMEM)] * (2 + len(arrays)),
        out_specs=pl.BlockSpec(memory_space=pltpu.VMEM),
        scratch_shapes=[
            pltpu.VMEM((len(arrays), rows, width), jnp.bfloat16),
            pltpu.VMEM((slots, points, points), jnp.bfloat16),
            pltpu.VMEM((slots, points, width), jnp.bfloat16),
        ],
        compiler_params=pltpu.CompilerParams(vmem_limit_bytes=VMEM_LIMIT),
    )(
        pltpu.with_memory_space_constraint(labels, pltpu.SMEM),
        in_vmem(blocks),
        in_vmem(other),
        *[in_vmem(array) for array in arrays],
    )


def swap(array, mask, count):
    return lax.ppermute(array, AXES, [(i, i ^ mask) for i in range(count)])


def gather(packed, count, blocks, codes):
    y, x, near = 2, 4, 8
    far = [1 << n for n in range(3, count.bit_length() - 1)]
    column = {0: packed}
    for bit in reversed(far):
        for mask, array in list(column.items()):
            if bit == near and mask == far[-1]:
                array, blocks = lax.optimization_barrier((array, blocks))
            column[mask ^ bit] = swap(array, bit, count)
    found = dict(column)
    for mask in sorted(column):
        if mask & near and mask != near:
            over_x, over_y = (swap(found[mask ^ near ^ bit], near, count) for bit in (x, y))
        else:
            over_x, over_y = (swap(column[mask], bit, count) for bit in (x, y))
        sent = over_x if mask & near else over_y
        if mask == 0:
            sent, codes = lax.optimization_barrier((sent, codes))
        corner = swap(sent, y if mask & near else x, count)
        found.update({mask ^ x: over_x, mask ^ y: over_y, mask ^ x ^ y: corner})
    return sorted(found.items()), blocks, codes


def total(values):
    while len(values) > 1:
        values = [values[n] + values[n + 1] for n in range(0, len(values), 2)]
    return values[0]


def shards(orbitals, occupied, panel_index, screening, block_region, block_row, block_col):
    groups, regions = lax.axis_size("grp"), lax.axis_size("reg")
    count = groups * regions
    points, occ_count = screening.shape[1], occupied.shape[2]

    other = swap(screening, 1, count)
    codes = (block_col * groups + block_row) * regions + block_region[:, 0]
    codes = (codes, swap(codes, 1, count))
    packed = pack(panel_index, orbitals[0, 0], occupied[0, 0])
    found, other, codes = gather(packed, count, other, codes)
    labels, blocks = collect(codes, screening, regions // 2)
    sums = partial_sigma(labels, blocks, other, found, regions // 2, points, occ_count)
    top = count // 2
    stage = []
    for far in (0, top):
        for mask in range(0, regions, 2):
            part = sums[mask // 2]
            stage.append(swap(part, far ^ mask, count) if far ^ mask else part)
    sigma = total(stage)
    bit = regions
    while bit < top:
        end = min(4 * bit, top)
        sigma = total([sigma] + [swap(sigma, mask, count) for mask in range(bit, end, bit)])
        bit = end
    return sigma[None]


def solution(mesh):
    in_specs = (
        P("reg", "grp", None, None),
        P("reg", "grp", None, None),
        P(),
        P(("grp", "reg"), None, None),
        P(("grp", "reg"), None),
        P(("grp", "reg")),
        P(("grp", "reg")),
    )
    out_specs = P("reg", None, None)
    return jax.shard_map(shards, mesh=mesh, in_specs=in_specs, out_specs=out_specs, check_vma=False)
```
